256 devices in a mesh: seq: 64 (over z, y, core), head: 4 (over x).
Axes of the slice: x: 4, y: 4, z: 8, core: 2. Of those that a mesh axis runs over, the one named last changes fastest.
Arguments:
- query: bfloat16 [256, 5120], P(('seq', 'head')), may hold values from -48 to 48
- query_tangent: bfloat16 [256, 5120], P(('seq', 'head')), may hold values from -6 to 6
- keys: bfloat16 [16384, 5120], P('seq', 'head'), may hold values from -4 to 4
- values: bfloat16 [16384, 5120], P('seq', 'head'), may hold values from -18 to 18
- key_tangent: bfloat16 [16384, 5120], P('seq', 'head'), may hold values from -6 to 6
- value_tangent: bfloat16 [16384, 5120], P('seq', 'head'), may hold values from -6 to 6
Outputs:
- attended: float32 [256, 5120], P('seq', 'head')
- attended_tangent: float32 [256, 5120], P('seq', 'head')
- lse: float32 [40, 256], P('head', 'seq')
- lse_tangent: float32 [40, 256], P('head', 'seq')
The draws below stay inside these ranges and needn't reach their ends.
All inputs are finite; a program needn't handle non-finite values.
Results may differ from the reference program's by a relative error of at most 0.012.
Values may be sent and summed in bfloat16 or wider, within the bound.
No kernel may reach another device: no remote copies, remote signals or barrier semaphores. Data moves between devices by JAX's collectives and lax.ppermute only.
A program may use at most 320 MiB of HBM per device.

```python
import math
import jax
import jax.numpy as jnp
from jax import lax

HEADS = 40
HD = 128
KEY_DEV = 256
WIN = 256
D = 5120
SEQ = 16384
N_SEQ = 64


def draw_keys(key, part):
    key = jax.random.fold_in(key, 3)
    result = jnp.clip(jax.random.normal(key, (SEQ, HEADS * HD), jnp.float32), -4.0, 4.0)
    return result.astype(jnp.bfloat16)


def draw_query(key, part):
    key = jax.random.fold_in(key, 5)
    window = jnp.clip(2.2 * jax.random.normal(key, (WIN, HEADS * HD), jnp.float32), -8.8, 8.8)
    return window.astype(jnp.bfloat16)


def block_scale(key, shape, cuts, low, high):
    gain = 1.0
    for dim, parts in cuts:
        draws = jax.random.uniform(jax.random.fold_in(jax.random.fold_in(key, 6), dim), (parts,), jnp.float32, low / len(cuts), high / len(cuts))
        gain = gain * jnp.repeat(jnp.exp(draws), shape[dim] // parts).reshape((-1,) + (1,) * (len(shape) - 1 - dim))
    return gain


def centred(rng, dims, spread, most, shards=(), kind=jnp.bfloat16):
    entries = jax.random.normal(rng, dims, jnp.float32) * spread
    if len(shards) > 0:
        entries = block_scale(rng, dims, shards, -0.22, 0.18) * entries
    return jnp.clip(entries, min=-most, max=most).astype(kind)


def setup_inputs(seed: int = 0) -> dict:
    splits = jax.random.split(jax.random.key(seed), 7)
    return {
        "query": draw_query(jax.random.fold_in(splits[6], 71), 0),
        "query_tangent": centred(splits[1], (WIN, D), 1.0, 6.0, ((0, 256),)),
        "keys": draw_keys(jax.random.fold_in(splits[6], 71), 0),
        "values": centred(splits[3], (SEQ, D), 3.0, 18.0, ((0, 64), (1, 4))),
        "key_tangent": centred(splits[4], (SEQ, D), 1.0, 6.0, ((0, 64), (1, 4))),
        "value_tangent": centred(splits[5], (SEQ, D), 1.0, 6.0, ((0, 64), (1, 4))),
    }


def block_terms(window, window_tangent, key_block, value_block, key_tangent_block, value_tangent_block):
    factor = 1.0 / math.sqrt(HD)
    scores = jnp.dot(window, key_block.T, preferred_element_type=jnp.float32) * factor
    score_tangent = (jnp.dot(window_tangent, key_block.T, preferred_element_type=jnp.float32) + jnp.dot(window, key_tangent_block.T, preferred_element_type=jnp.float32)) * factor
    block_max = lax.optimization_barrier(jnp.max(scores, axis=1))
    weights = jnp.exp(scores - block_max[:, None])
    rounded = weights.astype(jnp.bfloat16)
    product = weights * score_tangent
    tangent_weights = product.astype(jnp.bfloat16)
    block_total = lax.optimization_barrier(jnp.sum(weights, axis=1))
    block_slope = lax.optimization_barrier(jnp.sum(product, axis=1))
    block_out = jnp.dot(rounded, value_block, preferred_element_type=jnp.float32)
    block_out_tangent = jnp.dot(tangent_weights, value_block, preferred_element_type=jnp.float32) + jnp.dot(rounded, value_tangent_block, preferred_element_type=jnp.float32)
    return (block_out, block_out_tangent, block_total, block_slope, block_max)

def reference(query, query_tangent, keys, values, key_tangent, value_tangent):

    def one_head(head_index):
        column_start = head_index * HD

        def column_slice(array):
            return lax.dynamic_slice_in_dim(array, column_start, HD, 1)
        window = column_slice(query)
        window_tangent = column_slice(query_tangent)

        def blocked(array):
            return column_slice(array).reshape(N_SEQ, KEY_DEV, HD)

        def one_block(pieces):
            return block_terms(window, window_tangent, pieces[0], pieces[1], pieces[2], pieces[3])
        outs, outs_tangent, totals, slopes, maxima = lax.map(one_block, (blocked(keys), blocked(values), blocked(key_tangent), blocked(value_tangent)))
        top = lax.optimization_barrier(jnp.max(maxima, axis=0))
        scaling = jnp.exp(maxima - top[None, :])
        total = lax.optimization_barrier(jnp.sum(scaling * totals, axis=0))
        slope = lax.optimization_barrier(jnp.sum(scaling * slopes, axis=0))
        summed_out = lax.optimization_barrier(jnp.sum(scaling[:, :, None] * outs, axis=0))
        summed_tangent = lax.optimization_barrier(jnp.sum(scaling[:, :, None] * outs_tangent, axis=0))
        attended = summed_out / total[:, None]
        lse_tangent = slope / total
        attended_tangent = summed_tangent / total[:, None] - lse_tangent[:, None] * attended
        lse = top + jnp.log(total)
        return (attended, attended_tangent, lse, lse_tangent)
    attended, attended_tangent, lse, lse_tangent = lax.map(one_head, jnp.arange(HEADS, dtype=jnp.int32))
    attended = jnp.transpose(attended, (1, 0, 2)).reshape(WIN, HEADS * HD)
    attended_tangent = jnp.transpose(attended_tangent, (1, 0, 2)).reshape(WIN, HEADS * HD)
    return (attended, attended_tangent, lse, lse_tangent)
```

```python
import math

import jax
import jax.numpy as jnp
from jax import lax
from jax.experimental import pallas as pl
from jax.experimental.pallas import tpu as pltpu
from jax.sharding import Mesh, PartitionSpec as P

HD = 128
PAIR = 2
LANES = 128
LSE_PARTS = (0, 16, 32)
LT_PARTS = (48, 64, 80)

NT = (((1,), (1,)), ((), ()))


def split3(x):
    hi = x.astype(jnp.bfloat16).astype(jnp.float32)
    mid = (x - hi).astype(jnp.bfloat16).astype(jnp.float32)
    return hi, mid, x - hi - mid


def attend_kernel(
    owners, q_ref, k0, v0, kt0, vt0, k1, v1, kt1, vt1, msg_ref, lse_ref, lt_ref
):
    pair = pl.program_id(0)
    rows = q_ref.shape[1]
    per_owner = rows // owners
    lane = lax.broadcasted_iota(jnp.int32, (rows, LANES), 1)

    @pl.when(pair == 0)
    def _():
        lse_ref[...] = jnp.zeros_like(lse_ref)
        lt_ref[...] = jnp.zeros_like(lt_ref)

    factor = 1.0 / math.sqrt(HD)
    tiles = []
    for i in range(PAIR):
        cols = slice(i * HD, (i + 1) * HD)
        q = q_ref[0, :, cols]
        qt = q_ref[1, :, cols]

        def nt(a, b):
            return lax.dot_general(a, b, NT, preferred_element_type=jnp.float32)

        def nn(a, b):
            return jnp.dot(a, b, preferred_element_type=jnp.float32)

        blocks = [
            (k[:, cols], v[:, cols], kt[:, cols], vt[:, cols])
            for k, v, kt, vt in ((k0, v0, kt0, vt0), (k1, v1, kt1, vt1))
        ]
        scores = [nt(q, k) * factor for k, v, kt, vt in blocks]
        tangents = [(nt(qt, k) + nt(q, kt)) * factor for k, v, kt, vt in blocks]
        top = jnp.max(jnp.maximum(scores[0], scores[1]), axis=1, keepdims=True)
        weights = [jnp.exp(s - top) for s in scores]
        products = [w * t for w, t in zip(weights, tangents)]
        total = jnp.sum(weights[0] + weights[1], axis=1, keepdims=True)
        slope = jnp.sum(products[0] + products[1], axis=1, keepdims=True)
        out = jnp.zeros((rows, HD), jnp.float32)
        out_tangent = jnp.zeros((rows, HD), jnp.float32)
        for w, p, (k, v, kt, vt) in zip(weights, products, blocks):
            rounded = w.astype(jnp.bfloat16)
            out += nn(rounded, v)
            out_tangent += nn(p.astype(jnp.bfloat16), v) + nn(rounded, vt)
        inverse = 1.0 / total
        lt = slope * inverse
        out = out * inverse
        out_tangent = out_tangent * inverse - lt * out
        head = pair * PAIR + i
        lse_ref[...] = jnp.where(lane == head, top + jnp.log(total), lse_ref[...])
        lt_ref[...] = jnp.where(lane == head, lt, lt_ref[...])
        tiles += [
            out.reshape(owners, per_owner, HD),
            out_tangent.reshape(owners, per_owner, HD),
        ]
    tile = jnp.concatenate(tiles, axis=1)
    span = tile.shape[1]
    msg_ref[:, pl.ds(pl.multiple_of(pair * span, span), span), :] = tile.astype(jnp.bfloat16)

    @pl.when(pair == pl.num_programs(0) - 1)
    def _():
        stats = jnp.zeros((rows, LANES), jnp.float32)
        for ref, offsets in ((lse_ref, LSE_PARTS), (lt_ref, LT_PARTS)):
            for part, offset in zip(split3(ref[...]), offsets):
                stats += pltpu.roll(part, offset, 1) if offset else part
        stats = stats.reshape(owners, per_owner, LANES)
        stats = jnp.concatenate([stats, stats], axis=1)
        start = span * pl.num_programs(0)
        msg_ref[:, pl.ds(pl.multiple_of(start, 16), 2 * per_owner), :] = stats.astype(jnp.bfloat16)


def attend(window, own, other, owners):
    arrays, rows, width = window.shape
    keys = own[0].shape[0]
    per_owner = rows // owners
    heads = width // HD
    message_rows = (heads + 1) * 2 * per_owner
    block = PAIR * HD
    kv_spec = pl.BlockSpec((keys, block), lambda i: (0, i))
    return pl.pallas_call(
        lambda *refs: attend_kernel(owners, *refs),
        grid=(heads // PAIR,),
        out_shape=jax.ShapeDtypeStruct((owners, message_rows, HD), jnp.bfloat16),
        in_specs=[pl.BlockSpec((arrays, rows, block), lambda i: (0, 0, i))] + [kv_spec] * 8,
        out_specs=pl.BlockSpec((owners, message_rows, HD), lambda i: (0, 0, 0)),
        scratch_shapes=[pltpu.VMEM((rows, LANES), jnp.float32)] * 2,
        compiler_params=pltpu.CompilerParams(vmem_limit_bytes=24 * 1024 * 1024),
        cost_estimate=pl.CostEstimate(
            flops=12 * rows * 2 * keys * width,
            bytes_accessed=16 * keys * width,
            transcendentals=rows * 2 * keys * heads,
        ),
    )(window, *own, *other)


def merge_kernel(heads, msg_ref, out_ref, out_tangent_ref, lse_ref, lt_ref):
    owners = msg_ref.shape[0]
    half = out_ref.shape[0]
    span = 2 * half
    stats = msg_ref[:, heads * span : (heads + 1) * span, :].astype(jnp.float32)

    def gather_parts(offsets):
        total = None
        for offset in offsets[::-1]:
            part = pltpu.roll(stats, LANES - offset, 2) if offset else stats
            total = part if total is None else total + part
        return total

    lse_parts = gather_parts(LSE_PARTS)
    lt_parts = gather_parts(LT_PARTS)
    top = jnp.max(lse_parts, axis=0)
    weights = jnp.exp(lse_parts - top)
    total = jnp.sum(weights, axis=0)
    weights = weights * (1.0 / total)
    lse = top + jnp.log(total)
    lt = jnp.sum(weights * lt_parts, axis=0)
    shifts = weights * (lt_parts - lt)
    for head in range(heads):
        rows = slice(head * span, (head + 1) * span)
        values = msg_ref[:, rows, :].astype(jnp.float32)
        merged = jnp.sum(values * weights[:, :, head : head + 1], axis=0)
        moved = jnp.sum(values * shifts[:, :, head : head + 1], axis=0)
        cols = slice(head * HD, (head + 1) * HD)
        out_ref[:, cols] = merged[:half]
        out_tangent_ref[:, cols] = merged[half:] + moved[:half]
    lse_ref[...] = lse[:half, :heads]
    lt_ref[...] = lt[:half, :heads]


def merge(messages, heads):
    owners, message_rows, _ = messages.shape
    half = message_rows // (heads + 1) // 2
    vmem = pl.BlockSpec(memory_space=pltpu.VMEM)
    wide = jax.ShapeDtypeStruct((half, heads * HD), jnp.float32)
    small = jax.ShapeDtypeStruct((half, heads), jnp.float32)
    attended, attended_tangent, lse, lse_tangent = pl.pallas_call(
        lambda *refs: merge_kernel(heads, *refs),
        out_shape=(wide, wide, small, small),
        in_specs=[vmem],
        out_specs=(vmem,) * 4,
        compiler_params=pltpu.CompilerParams(vmem_limit_bytes=24 * 1024 * 1024),
    )(messages)
    return attended, attended_tangent, lse.T, lse_tangent.T


def per_device(query, query_tangent, keys, values, key_tangent, value_tangent):
    own = (keys, values, key_tangent, value_tangent)
    other = tuple(lax.ppermute(array, "core", [(0, 1), (1, 0)]) for array in own)
    owners = lax.axis_size("chip")
    groups = lax.axis_size("x")
    heads = keys.shape[1] // HD
    row = jnp.stack(
        [query.reshape(groups, heads * HD), query_tangent.reshape(groups, heads * HD)], axis=1
    )
    row = jnp.broadcast_to(row[None], (owners, *row.shape)).reshape(-1, 2, heads * HD)
    window = lax.all_to_all(row, ("chip", "x"), split_axis=0, concat_axis=0, tiled=True)
    window = jnp.transpose(window, (1, 0, 2))
    messages = attend(window, own, other, owners)
    messages = lax.all_to_all(messages, "chip", split_axis=0, concat_axis=0, tiled=True)
    return merge(messages, heads)


def solution(mesh):
    seq, head = mesh.devices.shape
    grid = Mesh(mesh.devices.reshape(seq // 2, 2, head), ("chip", "core", "x"))
    return jax.shard_map(
        per_device,
        mesh=grid,
        in_specs=(P(("chip", "core", "x"), None),) * 2 + (P(("chip", "core"), "x"),) * 4,
        out_specs=(P(("chip", "core"), "x"),) * 2 + (P("x", ("chip", "core")),) * 2,
        check_vma=False,
    )
```

```python
import math

import jax
import jax.numpy as jnp
from jax import lax
from jax.experimental import pallas as pl
from jax.experimental.pallas import tpu as pltpu
from jax.sharding import Mesh, PartitionSpec as P

HD = 128
LANES = 128
CORES = 2
Y = 4
NT = (((1,), (1,)), ((), ()))
VMEM_LIMIT = 32 * 1024 * 1024


def nt(a, b):
    return lax.dot_general(a, b, NT, preferred_element_type=jnp.float32)


def nn(a, b):
    return jnp.dot(a, b, preferred_element_type=jnp.float32)


def split3(x):
    hi = x.astype(jnp.bfloat16).astype(jnp.float32)
    mid = (x - hi).astype(jnp.bfloat16).astype(jnp.float32)
    return hi, mid, x - hi - mid


def encode(lse, lt, heads):
    total = None
    for i, part in enumerate((*split3(lse), *split3(lt))):
        part = pltpu.roll(part, i * heads, part.ndim - 1) if i else part
        total = part if total is None else total + part
    return total


def decode(stats, heads):
    parts = [
        pltpu.roll(stats, LANES - i * heads, stats.ndim - 1) if i else stats for i in range(6)
    ]
    return parts[2] + parts[1] + parts[0], parts[5] + parts[4] + parts[3]


def twice(x):
    return jnp.concatenate([x, x], axis=1)


def attend_kernel(owners, groups, *refs):
    windows, keys, outs = refs[:groups], refs[groups : groups + 8], refs[groups + 8 :]
    rows = windows[0].shape[1]
    total_rows = rows * groups
    heads = windows[0].shape[2] // HD
    per_owner = rows // owners
    factor = 1.0 / math.sqrt(HD)
    lane = lax.broadcasted_iota(jnp.int32, (total_rows, LANES), 1)
    lses = jnp.zeros((total_rows, LANES), jnp.float32)
    lts = jnp.zeros((total_rows, LANES), jnp.float32)
    pending = None
    for head in range(heads):
        cols = slice(head * HD, (head + 1) * HD)
        q = jnp.concatenate([w[0, :, cols] for w in windows], axis=0)
        qt = jnp.concatenate([w[1, :, cols] for w in windows], axis=0)
        blocks = [tuple(ref[:, cols] for ref in keys[i : i + 4]) for i in (0, 4)]
        scores = [nt(q, k) * factor for k, v, kt, vt in blocks]
        tangents = [(nt(qt, k) + nt(q, kt)) * factor for k, v, kt, vt in blocks]
        top = jnp.max(jnp.maximum(scores[0], scores[1]), axis=1, keepdims=True)
        weights = [jnp.exp(s - top) for s in scores]
        products = [w * t for w, t in zip(weights, tangents)]
        total = jnp.sum(weights[0] + weights[1], axis=1, keepdims=True)
        slope = jnp.sum(products[0] + products[1], axis=1, keepdims=True)
        out = jnp.zeros((total_rows, HD), jnp.float32)
        out_tangent = jnp.zeros((total_rows, HD), jnp.float32)
        for w, p, (k, v, kt, vt) in zip(weights, products, blocks):
            rounded = w.astype(jnp.bfloat16)
            out += nn(rounded, v)
            out_tangent += nn(p.astype(jnp.bfloat16), v) + nn(rounded, vt)
        inverse = 1.0 / total
        lt = slope * inverse
        out = out * inverse
        out_tangent = out_tangent * inverse - lt * out
        lses = jnp.where(lane == head, top + jnp.log(total), lses)
        lts = jnp.where(lane == head, lt, lts)
        tile = jnp.concatenate(
            [
                out.reshape(groups * owners, per_owner, HD),
                out_tangent.reshape(groups * owners, per_owner, HD),
            ],
            axis=1,
        )
        if pending is None:
            pending = tile
            continue
        tile = jnp.concatenate([pending, tile], axis=1).astype(jnp.bfloat16)
        pending = None
        span = tile.shape[1]
        start = (head // 2) * span
        for i, ref in enumerate(outs):
            ref[:, start : start + span, :] = tile[i * owners : (i + 1) * owners]
    stats = twice(encode(lses, lts, heads).reshape(groups * owners, per_owner, LANES))
    span = stats.shape[1]
    for i, ref in enumerate(outs):
        part = stats[i * owners : (i + 1) * owners]
        ref[:, heads * span : (heads + 1) * span, :] = part.astype(jnp.bfloat16)


def attend(windows, own, other, owners):
    arrays, rows, width = windows[0].shape
    groups = len(windows)
    heads = width // HD
    message_rows = (heads + 1) * 2 * (rows // owners)
    vmem = pl.BlockSpec(memory_space=pltpu.VMEM)
    keys = own[0].shape[0] * 2
    return pl.pallas_call(
        lambda *refs: attend_kernel(owners, groups, *refs),
        out_shape=[jax.ShapeDtypeStruct((owners, message_rows, HD), jnp.bfloat16)] * groups,
        in_specs=[vmem] * (groups + 8),
        out_specs=[vmem] * groups,
        compiler_params=pltpu.CompilerParams(vmem_limit_bytes=VMEM_LIMIT),
        cost_estimate=pl.CostEstimate(
            flops=12 * rows * groups * keys * width,
            bytes_accessed=8 * keys * width,
            transcendentals=rows * groups * keys * heads,
        ),
    )(*windows, *own, *other)


def merge_weights(stats, heads):
    decoded = [decode(s.astype(jnp.float32), heads) for s in stats]
    top = decoded[0][0]
    for lse, _ in decoded[1:]:
        top = jnp.maximum(top, lse)
    scales = [jnp.exp(lse - top) for lse, _ in decoded]
    total = sum(scales[1:], scales[0])
    inverse = 1.0 / total
    scales = [scale * inverse for scale in scales]
    lt = sum(scale * part for scale, (_, part) in zip(scales, decoded))
    shifts = [scale * (part - lt) for scale, (_, part) in zip(scales, decoded)]
    return scales, shifts, top + jnp.log(total), lt


def merge_group_kernel(heads, *refs):
    sources, out_ref = refs[:-1], refs[-1]
    owners, message_rows, _ = out_ref.shape
    span = message_rows // (heads + 1)
    half = span // 2
    scales, shifts, lse, lt = merge_weights(
        [ref[:, heads * span : (heads + 1) * span, :] for ref in sources], heads
    )
    tangent_row = lax.broadcasted_iota(jnp.int32, (owners, span, HD), 1) >= half
    for pair in range(heads // 2):
        tiles = []
        for head in (2 * pair, 2 * pair + 1):
            rows = slice(head * span, (head + 1) * span)
            merged = moved = 0.0
            for ref, scale, shift in zip(sources, scales, shifts):
                values = ref[:, rows, :].astype(jnp.float32)
                merged += values * scale[:, :, head : head + 1]
                moved += values * shift[:, :, head : head + 1]
            moved = pltpu.roll(moved, half, 1)
            tiles.append(jnp.where(tangent_row, merged + moved, merged))
        start = pair * 2 * span
        tile = jnp.concatenate(tiles, axis=1).astype(jnp.bfloat16)
        out_ref[:, start : start + 2 * span, :] = tile
    lane = lax.broadcasted_iota(jnp.int32, lse.shape, 2)
    stats = encode(jnp.where(lane < heads, lse, 0.0), jnp.where(lane < heads, lt, 0.0), heads)
    out_ref[:, heads * span : (heads + 1) * span, :] = stats.astype(jnp.bfloat16)


def merge_group(messages, heads):
    vmem = pl.BlockSpec(memory_space=pltpu.VMEM)
    return pl.pallas_call(
        lambda *refs: merge_group_kernel(heads, *refs),
        out_shape=jax.ShapeDtypeStruct(messages[0].shape, jnp.bfloat16),
        in_specs=[vmem] * len(messages),
        out_specs=vmem,
        compiler_params=pltpu.CompilerParams(vmem_limit_bytes=VMEM_LIMIT),
    )(*messages)


def merge_kernel(heads, msg_ref, out_ref, out_tangent_ref, lse_ref, lt_ref):
    half = out_ref.shape[0]
    span = 2 * half
    stats = msg_ref[:, heads * span : (heads + 1) * span, :]
    count = msg_ref.shape[0]
    scales, shifts, lse, lt = merge_weights([stats[i] for i in range(count)], heads)
    for head in range(heads):
        rows = slice(head * span, (head + 1) * span)
        merged = moved = 0.0
        for i, (scale, shift) in enumerate(zip(scales, shifts)):
            values = msg_ref[i, rows, :].astype(jnp.float32)
            merged += values * scale[:, head : head + 1]
            moved += values * shift[:, head : head + 1]
        cols = slice(head * HD, (head + 1) * HD)
        out_ref[:, cols] = merged[:half]
        out_tangent_ref[:, cols] = merged[half:] + moved[:half]
    lse_ref[...] = lse[:half, :heads]
    lt_ref[...] = lt[:half, :heads]


def merge(messages, heads):
    half = messages.shape[1] // (heads + 1) // 2
    vmem = pl.BlockSpec(memory_space=pltpu.VMEM)
    wide = jax.ShapeDtypeStruct((half, heads * HD), jnp.float32)
    small = jax.ShapeDtypeStruct((half, heads), jnp.float32)
    attended, attended_tangent, lse, lse_tangent = pl.pallas_call(
        lambda *refs: merge_kernel(heads, *refs),
        out_shape=(wide, wide, small, small),
        in_specs=[vmem],
        out_specs=(vmem,) * 4,
        compiler_params=pltpu.CompilerParams(vmem_limit_bytes=VMEM_LIMIT),
    )(messages)
    return attended, attended_tangent, lse.T, lse_tangent.T


def shift(array, step):
    count = lax.axis_size("y")
    return lax.ppermute(array, "y", [(i, (i + step) % count) for i in range(count)])


def per_device(query, query_tangent, keys, values, key_tangent, value_tangent):
    own = (keys, values, key_tangent, value_tangent)
    other = tuple(lax.ppermute(array, "core", [(0, 1), (1, 0)]) for array in own)
    owners = lax.axis_size("z")
    heads = keys.shape[1] // HD
    row = jnp.stack(
        [array.reshape(lax.axis_size("x"), heads * HD) for array in (query, query_tangent)], axis=1
    )
    row = jnp.broadcast_to(row[None], (owners, *row.shape)).reshape(-1, 2, heads * HD)
    window = lax.all_to_all(row, ("z", "x"), split_axis=0, concat_axis=0, tiled=True)
    window = jnp.transpose(window, (1, 0, 2))
    steps = (1, 3, 2)
    windows = [window] + [shift(window, step) for step in steps]
    messages = attend(windows, own, other, owners)
    messages = [messages[0]] + [shift(m, -step) for m, step in zip(messages[1:], steps)]
    message = merge_group(messages, heads)
    message = lax.all_to_all(message, "z", split_axis=0, concat_axis=0, tiled=True)
    return merge(message, heads)


def solution(mesh):
    seq, head = mesh.devices.shape
    devices = mesh.devices.reshape(seq // (Y * CORES), Y, CORES, head)
    seq_axes = ("z", "y", "core")
    return jax.shard_map(
        per_device,
        mesh=Mesh(devices, (*seq_axes, "x")),
        in_specs=(P((*seq_axes, "x"), None),) * 2 + (P(seq_axes, "x"),) * 4,
        out_specs=(P(seq_axes, "x"),) * 2 + (P("x", seq_axes),) * 2,
        check_vma=False,
    )
```

```python
import math

import jax
import jax.numpy as jnp
from jax import lax
from jax.experimental import pallas as pl
from jax.experimental.pallas import tpu as pltpu
from jax.sharding import Mesh, PartitionSpec as P

HD = 128
LANES = 128
CORES = 2
Y = 4
NT = (((1,), (1,)), ((), ()))
VMEM_LIMIT = 32 * 1024 * 1024


def nt(a, b):
    return lax.dot_general(a, b, NT, preferred_element_type=jnp.float32)


def nn(a, b):
    return jnp.dot(a, b, preferred_element_type=jnp.float32)


def split3(x):
    hi = x.astype(jnp.bfloat16).astype(jnp.float32)
    mid = (x - hi).astype(jnp.bfloat16).astype(jnp.float32)
    return hi, mid, x - hi - mid


def encode(lse, lt, heads):
    total = None
    for i, part in enumerate((*split3(lse), *split3(lt))):
        part = pltpu.roll(part, i * heads, part.ndim - 1) if i else part
        total = part if total is None else total + part
    return total


def decode(stats, heads):
    parts = [
        pltpu.roll(stats, LANES - i * heads, stats.ndim - 1) if i else stats for i in range(6)
    ]
    return parts[2] + parts[1] + parts[0], parts[5] + parts[4] + parts[3]


def twice(x):
    return jnp.concatenate([x, x], axis=1)


LOADS = 2


def spread_kernel(copies, groups, q_ref, qt_ref, out_ref):
    width = q_ref.shape[1] // groups
    for group in range(groups):
        cols = slice(group * width, (group + 1) * width)
        pair = jnp.concatenate([q_ref[:, cols], qt_ref[:, cols]], axis=0)
        for copy in range(copies):
            out_ref[copy * groups + group] = pair


def spread(query, query_tangent, copies, groups):
    width = query.shape[1] // groups
    vmem = pl.BlockSpec(memory_space=pltpu.VMEM)
    return pl.pallas_call(
        lambda *refs: spread_kernel(copies, groups, *refs),
        out_shape=jax.ShapeDtypeStruct((copies * groups, 2, width), query.dtype),
        in_specs=[vmem] * 2,
        out_specs=vmem,
        compiler_params=pltpu.CompilerParams(vmem_limit_bytes=VMEM_LIMIT),
    )(query, query_tangent)


def load_kernel(*refs):
    count = (len(refs) - 1) // 2
    sources, targets, sems = refs[:count], refs[count : 2 * count], refs[-1]
    copies = []
    for i, (source, target) in enumerate(zip(sources, targets)):
        rows = source.shape[0] // LOADS
        for j in range(LOADS):
            part = pl.ds(j * rows, rows)
            copies.append(
                pltpu.make_async_copy(source.at[part], target.at[part], sems.at[i * LOADS + j])
            )
    for copy in copies:
        copy.start()
    for copy in copies:
        copy.wait()


def load(arrays):
    count = len(arrays)
    size = sum(array.size for array in arrays)
    return pl.pallas_call(
        load_kernel,
        out_shape=[jax.ShapeDtypeStruct(array.shape, array.dtype) for array in arrays],
        in_specs=[pl.BlockSpec(memory_space=pltpu.HBM)] * count,
        out_specs=[pl.BlockSpec(memory_space=pltpu.VMEM)] * count,
        scratch_shapes=[pltpu.SemaphoreType.DMA((count * LOADS,))],
        compiler_params=pltpu.CompilerParams(vmem_limit_bytes=VMEM_LIMIT),
        cost_estimate=pl.CostEstimate(flops=0, bytes_accessed=4 * size, transcendentals=0),
    )(*arrays)


def attend_kernel(owners, groups, *refs):
    windows, keys, outs = refs[:groups], refs[groups : groups + 8], refs[groups + 8 :]
    rows = windows[0].shape[1]
    total_rows = rows * groups
    heads = windows[0].shape[2] // HD
    per_owner = rows // owners
    factor = 1.0 / math.sqrt(HD)
    lane = lax.broadcasted_iota(jnp.int32, (total_rows, LANES), 1)
    lses = jnp.zeros((total_rows, LANES), jnp.float32)
    lts = jnp.zeros((total_rows, LANES), jnp.float32)
    pending = None
    for head in range(heads):
        cols = slice(head * HD, (head + 1) * HD)
        q = jnp.concatenate([w[0, :, cols] for w in windows], axis=0)
        qt = jnp.concatenate([w[1, :, cols] for w in windows], axis=0)
        blocks = [tuple(ref[:, cols] for ref in keys[i : i + 4]) for i in (0, 4)]
        scores = [nt(q, k) * factor for k, v, kt, vt in blocks]
        tangents = [(nt(qt, k) + nt(q, kt)) * factor for k, v, kt, vt in blocks]
        top = jnp.max(jnp.maximum(scores[0], scores[1]), axis=1, keepdims=True)
        weights = [jnp.exp(s - top) for s in scores]
        products = [w * t for w, t in zip(weights, tangents)]
        total = jnp.sum(weights[0] + weights[1], axis=1, keepdims=True)
        slope = jnp.sum(products[0] + products[1], axis=1, keepdims=True)
        out = jnp.zeros((total_rows, HD), jnp.float32)
        out_tangent = jnp.zeros((total_rows, HD), jnp.float32)
        for w, p, (k, v, kt, vt) in zip(weights, products, blocks):
            rounded = w.astype(jnp.bfloat16)
            out += nn(rounded, v)
            out_tangent += nn(p.astype(jnp.bfloat16), v) + nn(rounded, vt)
        inverse = 1.0 / total
        lt = slope * inverse
        out = out * inverse
        out_tangent = out_tangent * inverse - lt * out
        lses = jnp.where(lane == head, top + jnp.log(total), lses)
        lts = jnp.where(lane == head, lt, lts)
        tile = jnp.concatenate(
            [
                out.reshape(groups * owners, per_owner, HD),
                out_tangent.reshape(groups * owners, per_owner, HD),
            ],
            axis=1,
        )
        if pending is None:
            pending = tile
            continue
        tile = jnp.concatenate([pending, tile], axis=1).astype(jnp.bfloat16)
        pending = None
        span = tile.shape[1]
        start = (head // 2) * span
        for i, ref in enumerate(outs):
            ref[:, start : start + span, :] = tile[i * owners : (i + 1) * owners]
    stats = twice(encode(lses, lts, heads).reshape(groups * owners, per_owner, LANES))
    span = stats.shape[1]
    for i, ref in enumerate(outs):
        part = stats[i * owners : (i + 1) * owners]
        ref[:, heads * span : (heads + 1) * span, :] = part.astype(jnp.bfloat16)


def attend(windows, own, other, owners):
    arrays, rows, width = windows[0].shape
    groups = len(windows)
    heads = width // HD
    message_rows = (heads + 1) * 2 * (rows // owners)
    vmem = pl.BlockSpec(memory_space=pltpu.VMEM)
    keys = own[0].shape[0] * 2
    return pl.pallas_call(
        lambda *refs: attend_kernel(owners, groups, *refs),
        out_shape=[jax.ShapeDtypeStruct((owners, message_rows, HD), jnp.bfloat16)] * groups,
        in_specs=[vmem] * (groups + 8),
        out_specs=[vmem] * groups,
        compiler_params=pltpu.CompilerParams(vmem_limit_bytes=VMEM_LIMIT),
        cost_estimate=pl.CostEstimate(
            flops=12 * rows * groups * keys * width,
            bytes_accessed=8 * keys * width,
            transcendentals=rows * groups * keys * heads,
        ),
    )(*windows, *own, *other)


def merge_weights(stats, heads):
    decoded = [decode(s.astype(jnp.float32), heads) for s in stats]
    top = decoded[0][0]
    for lse, _ in decoded[1:]:
        top = jnp.maximum(top, lse)
    scales = [jnp.exp(lse - top) for lse, _ in decoded]
    total = sum(scales[1:], scales[0])
    inverse = 1.0 / total
    scales = [scale * inverse for scale in scales]
    lt = sum(scale * part for scale, (_, part) in zip(scales, decoded))
    shifts = [scale * (part - lt) for scale, (_, part) in zip(scales, decoded)]
    return scales, shifts, top + jnp.log(total), lt


def merge_group_kernel(heads, *refs):
    sources, out_ref = refs[:-1], refs[-1]
    owners, message_rows, _ = out_ref.shape
    span = message_rows // (heads + 1)
    half = span // 2
    scales, shifts, lse, lt = merge_weights(
        [ref[:, heads * span : (heads + 1) * span, :] for ref in sources], heads
    )
    tangent_row = lax.broadcasted_iota(jnp.int32, (owners, span, HD), 1) >= half
    for pair in range(heads // 2):
        tiles = []
        for head in (2 * pair, 2 * pair + 1):
            rows = slice(head * span, (head + 1) * span)
            merged = moved = 0.0
            for ref, scale, shift in zip(sources, scales, shifts):
                values = ref[:, rows, :].astype(jnp.float32)
                merged += values * scale[:, :, head : head + 1]
                moved += values * shift[:, :, head : head + 1]
            moved = pltpu.roll(moved, half, 1)
            tiles.append(jnp.where(tangent_row, merged + moved, merged))
        start = pair * 2 * span
        tile = jnp.concatenate(tiles, axis=1).astype(jnp.bfloat16)
        out_ref[:, start : start + 2 * span, :] = tile
    lane = lax.broadcasted_iota(jnp.int32, lse.shape, 2)
    stats = encode(jnp.where(lane < heads, lse, 0.0), jnp.where(lane < heads, lt, 0.0), heads)
    out_ref[:, heads * span : (heads + 1) * span, :] = stats.astype(jnp.bfloat16)


def merge_group(messages, heads):
    vmem = pl.BlockSpec(memory_space=pltpu.VMEM)
    return pl.pallas_call(
        lambda *refs: merge_group_kernel(heads, *refs),
        out_shape=jax.ShapeDtypeStruct(messages[0].shape, jnp.bfloat16),
        in_specs=[vmem] * len(messages),
        out_specs=vmem,
        compiler_params=pltpu.CompilerParams(vmem_limit_bytes=VMEM_LIMIT),
    )(*messages)


def merge_kernel(heads, msg_ref, out_ref, out_tangent_ref, lse_ref, lt_ref):
    half = out_ref.shape[0]
    span = 2 * half
    stats = msg_ref[:, heads * span : (heads + 1) * span, :]
    count = msg_ref.shape[0]
    scales, shifts, lse, lt = merge_weights([stats[i] for i in range(count)], heads)
    for head in range(heads):
        rows = slice(head * span, (head + 1) * span)
        merged = moved = 0.0
        for i, (scale, shift) in enumerate(zip(scales, shifts)):
            values = msg_ref[i, rows, :].astype(jnp.float32)
            merged += values * scale[:, head : head + 1]
            moved += values * shift[:, head : head + 1]
        cols = slice(head * HD, (head + 1) * HD)
        out_ref[:, cols] = merged[:half]
        out_tangent_ref[:, cols] = merged[half:] + moved[:half]
    lse_ref[...] = lse[:half, :heads]
    lt_ref[...] = lt[:half, :heads]


def merge(messages, heads):
    half = messages.shape[1] // (heads + 1) // 2
    vmem = pl.BlockSpec(memory_space=pltpu.VMEM)
    wide = jax.ShapeDtypeStruct((half, heads * HD), jnp.float32)
    small = jax.ShapeDtypeStruct((half, heads), jnp.float32)
    attended, attended_tangent, lse, lse_tangent = pl.pallas_call(
        lambda *refs: merge_kernel(heads, *refs),
        out_shape=(wide, wide, small, small),
        in_specs=[vmem],
        out_specs=(vmem,) * 4,
        compiler_params=pltpu.CompilerParams(vmem_limit_bytes=VMEM_LIMIT),
    )(messages)
    return attended, attended_tangent, lse.T, lse_tangent.T


def shift(array, step):
    count = lax.axis_size("y")
    return lax.ppermute(array, "y", [(i, (i + step) % count) for i in range(count)])


def per_device(query, query_tangent, keys, values, key_tangent, value_tangent):
    own = (keys, values, key_tangent, value_tangent)
    other = tuple(lax.ppermute(array, "core", [(0, 1), (1, 0)]) for array in own)
    owners = lax.axis_size("z")
    heads = keys.shape[1] // HD
    row = spread(query, query_tangent, owners, lax.axis_size("x"))
    row, own = lax.optimization_barrier((row, own))
    window = lax.all_to_all(row, ("z", "x"), split_axis=0, concat_axis=0, tiled=True)
    window = jnp.transpose(window, (1, 0, 2))
    window, own, other = lax.optimization_barrier((window, load(own), other))
    steps = (1, 3, 2)
    windows = [window] + [shift(window, step) for step in steps]
    messages = attend(windows, own, other, owners)
    messages = [messages[0]] + [shift(m, -step) for m, step in zip(messages[1:], steps)]
    message = merge_group(messages, heads)
    message = lax.all_to_all(message, "z", split_axis=0, concat_axis=0, tiled=True)
    return merge(message, heads)


def solution(mesh):
    seq, head = mesh.devices.shape
    devices = mesh.devices.reshape(seq // (Y * CORES), Y, CORES, head)
    seq_axes = ("z", "y", "core")
    return jax.shard_map(
        per_device,
        mesh=Mesh(devices, (*seq_axes, "x")),
        in_specs=(P((*seq_axes, "x"), None),) * 2 + (P(seq_axes, "x"),) * 4,
        out_specs=(P(seq_axes, "x"),) * 2 + (P("x", seq_axes),) * 2,
        check_vma=False,
    )
```

```python
import math

import jax
import jax.numpy as jnp
from jax import lax
from jax.experimental import pallas as pl
from jax.experimental.pallas import tpu as pltpu
from jax.sharding import Mesh, PartitionSpec as P

HD = 128
LANES = 128
CORES = 2
Y = 4
FIRST_HEADS = 4
NT = (((1,), (1,)), ((), ()))
VMEM_LIMIT = 32 * 1024 * 1024


def nt(a, b):
    return lax.dot_general(a, b, NT, preferred_element_type=jnp.float32)


def nn(a, b):
    return jnp.dot(a, b, preferred_element_type=jnp.float32)


def split3(x):
    hi = x.astype(jnp.bfloat16).astype(jnp.float32)
    mid = (x - hi).astype(jnp.bfloat16).astype(jnp.float32)
    return hi, mid, x - hi - mid


def encode(lse, lt, heads):
    total = None
    for i, part in enumerate((*split3(lse), *split3(lt))):
        part = pltpu.roll(part, i * heads, part.ndim - 1) if i else part
        total = part if total is None else total + part
    return total


def decode(stats, heads):
    parts = [
        pltpu.roll(stats, LANES - i * heads, stats.ndim - 1) if i else stats for i in range(6)
    ]
    return parts[2] + parts[1] + parts[0], parts[5] + parts[4] + parts[3]


def twice(x):
    return jnp.concatenate([x, x], axis=1)


def spread_kernel(copies, groups, row_ref, out_ref):
    width = row_ref.shape[1] // groups
    for group in range(groups):
        pair = row_ref[:, group * width : (group + 1) * width]
        for copy in range(copies):
            out_ref[copy * groups + group] = pair


def spread(row, copies, groups):
    arrays, width = row.shape
    vmem = pl.BlockSpec(memory_space=pltpu.VMEM)
    return pl.pallas_call(
        lambda *refs: spread_kernel(copies, groups, *refs),
        out_shape=jax.ShapeDtypeStruct((copies * groups, arrays, width // groups), row.dtype),
        in_specs=[vmem],
        out_specs=vmem,
        compiler_params=pltpu.CompilerParams(vmem_limit_bytes=VMEM_LIMIT),
    )(row)


def attend_kernel(owners, groups, first, last, *refs):
    windows, sources = refs[:groups], refs[groups : groups + 8]
    rest = refs[groups + 8 :]
    if first == 0:
        carried = None
    else:
        carried, rest = rest[:2], rest[2:]
    outs, rest = rest[:groups], rest[groups:]
    stats_out, (buffers, sems) = rest[:-2], rest[-2:]
    rows = windows[0].shape[1]
    total_rows = rows * groups
    heads = windows[0].shape[2] // HD
    per_owner = rows // owners
    factor = 1.0 / math.sqrt(HD)
    width = 2 * HD
    copies = []
    for pair in range(heads // 2):
        copies.append(
            [
                pltpu.make_async_copy(
                    source.at[:, pl.ds(first * HD + pair * width, width)],
                    buffers.at[i, :, pl.ds(pair * width, width)],
                    sems.at[i, pair],
                )
                for i, source in enumerate(sources)
            ]
        )
        for copy in copies[-1]:
            copy.start()
    lane = lax.broadcasted_iota(jnp.int32, (total_rows, LANES), 1)
    if carried is None:
        lses = jnp.zeros((total_rows, LANES), jnp.float32)
        lts = jnp.zeros((total_rows, LANES), jnp.float32)
    else:
        lses, lts = carried[0][...], carried[1][...]
    pending = None
    for head in range(heads):
        cols = slice(head * HD, (head + 1) * HD)
        if head % 2 == 0:
            for copy in copies[head // 2]:
                copy.wait()
        q = jnp.concatenate([w[0, :, cols] for w in windows], axis=0)
        qt = jnp.concatenate([w[1, :, cols] for w in windows], axis=0)
        blocks = [tuple(buffers[j, :, cols] for j in range(i, i + 4)) for i in (0, 4)]
        scores = [nt(q, k) * factor for k, v, kt, vt in blocks]
        tangents = [(nt(qt, k) + nt(q, kt)) * factor for k, v, kt, vt in blocks]
        top = jnp.max(jnp.maximum(scores[0], scores[1]), axis=1, keepdims=True)
        weights = [jnp.exp(s - top) for s in scores]
        products = [w * t for w, t in zip(weights, tangents)]
        total = jnp.sum(weights[0] + weights[1], axis=1, keepdims=True)
        slope = jnp.sum(products[0] + products[1], axis=1, keepdims=True)
        out = jnp.zeros((total_rows, HD), jnp.float32)
        out_tangent = jnp.zeros((total_rows, HD), jnp.float32)
        for w, p, (k, v, kt, vt) in zip(weights, products, blocks):
            rounded = w.astype(jnp.bfloat16)
            out += nn(rounded, v)
            out_tangent += nn(p.astype(jnp.bfloat16), v) + nn(rounded, vt)
        inverse = 1.0 / total
        lt = slope * inverse
        out = out * inverse
        out_tangent = out_tangent * inverse - lt * out
        lses = jnp.where(lane == first + head, top + jnp.log(total), lses)
        lts = jnp.where(lane == first + head, lt, lts)
        tile = jnp.concatenate(
            [
                out.reshape(groups * owners, per_owner, HD),
                out_tangent.reshape(groups * owners, per_owner, HD),
            ],
            axis=1,
        )
        if pending is None:
            pending = tile
            continue
        tile = jnp.concatenate([pending, tile], axis=1).astype(jnp.bfloat16)
        pending = None
        span = tile.shape[1]
        start = (head // 2) * span
        for i, ref in enumerate(outs):
            ref[:, start : start + span, :] = tile[i * owners : (i + 1) * owners]
    if not last:
        stats_out[0][...] = lses
        stats_out[1][...] = lts
        return
    stats = encode(lses, lts, first + heads)
    stats = twice(stats.reshape(groups * owners, per_owner, LANES))
    span = stats.shape[1]
    for i, ref in enumerate(outs):
        part = stats[i * owners : (i + 1) * owners]
        ref[:, heads * span : (heads + 1) * span, :] = part.astype(jnp.bfloat16)


def attend(windows, own, other, owners, first, last, carried):
    arrays, rows, width = windows[0].shape
    groups = len(windows)
    heads = width // HD
    total_rows = rows * groups
    message_rows = (heads + last) * 2 * (rows // owners)
    vmem = pl.BlockSpec(memory_space=pltpu.VMEM)
    keys = own[0].shape[0]
    outs = [jax.ShapeDtypeStruct((owners, message_rows, HD), jnp.bfloat16)] * groups
    if not last:
        outs += [jax.ShapeDtypeStruct((total_rows, LANES), jnp.float32)] * 2
    result = pl.pallas_call(
        lambda *refs: attend_kernel(owners, groups, first, last, *refs),
        out_shape=outs,
        in_specs=[vmem] * groups
        + [pl.BlockSpec(memory_space=pl.ANY)] * 8
        + [vmem] * len(carried),
        out_specs=[vmem] * len(outs),
        scratch_shapes=[
            pltpu.VMEM((8, keys, width), jnp.bfloat16),
            pltpu.SemaphoreType.DMA((8, heads // 2)),
        ],
        cost_estimate=pl.CostEstimate(
            flops=24 * total_rows * keys * width,
            bytes_accessed=16 * keys * width,
            transcendentals=2 * total_rows * keys * heads,
        ),
    )(*windows, *own, *other, *carried)
    return result[:groups], result[groups:]


def merge_weights(stats, heads):
    decoded = [decode(s.astype(jnp.float32), heads) for s in stats]
    top = decoded[0][0]
    for lse, _ in decoded[1:]:
        top = jnp.maximum(top, lse)
    scales = [jnp.exp(lse - top) for lse, _ in decoded]
    total = sum(scales[1:], scales[0])
    inverse = 1.0 / total
    scales = [scale * inverse for scale in scales]
    lt = sum(scale * part for scale, (_, part) in zip(scales, decoded))
    shifts = [scale * (part - lt) for scale, (_, part) in zip(scales, decoded)]
    return scales, shifts, top + jnp.log(total), lt


def merge_group_kernel(splits, groups, *refs):
    parts, out_ref = refs[:-1], refs[-1]
    parts = [parts[i * groups : (i + 1) * groups] for i in range(len(splits))]
    heads = sum(splits)
    owners, message_rows, _ = out_ref.shape
    span = message_rows // (heads + 1)
    half = span // 2
    last = splits[-1]
    scales, shifts, lse, lt = merge_weights(
        [ref[:, last * span : (last + 1) * span, :] for ref in parts[-1]], heads
    )
    tangent_row = lax.broadcasted_iota(jnp.int32, (owners, span, HD), 1) >= half
    places = [(part, head) for part, count in zip(parts, splits) for head in range(count)]
    for pair in range(heads // 2):
        tiles = []
        for head in (2 * pair, 2 * pair + 1):
            sources, place = places[head]
            rows = slice(place * span, (place + 1) * span)
            merged = moved = 0.0
            for ref, scale, shift in zip(sources, scales, shifts):
                values = ref[:, rows, :].astype(jnp.float32)
                merged += values * scale[:, :, head : head + 1]
                moved += values * shift[:, :, head : head + 1]
            moved = pltpu.roll(moved, half, 1)
            tiles.append(jnp.where(tangent_row, merged + moved, merged))
        start = pair * 2 * span
        tile = jnp.concatenate(tiles, axis=1).astype(jnp.bfloat16)
        out_ref[:, start : start + 2 * span, :] = tile
    lane = lax.broadcasted_iota(jnp.int32, lse.shape, 2)
    stats = encode(jnp.where(lane < heads, lse, 0.0), jnp.where(lane < heads, lt, 0.0), heads)
    out_ref[:, heads * span : (heads + 1) * span, :] = stats.astype(jnp.bfloat16)


def merge_group(parts, splits):
    vmem = pl.BlockSpec(memory_space=pltpu.VMEM)
    groups = len(parts[0])
    owners, rows, lanes = parts[0][0].shape
    rows = rows // splits[0] * (sum(splits) + 1)
    messages = [message for part in parts for message in part]
    return pl.pallas_call(
        lambda *refs: merge_group_kernel(splits, groups, *refs),
        out_shape=jax.ShapeDtypeStruct((owners, rows, lanes), jnp.bfloat16),
        in_specs=[vmem] * len(messages),
        out_specs=vmem,
        compiler_params=pltpu.CompilerParams(vmem_limit_bytes=VMEM_LIMIT),
    )(*messages)


def merge_kernel(heads, msg_ref, out_ref, out_tangent_ref, lse_ref, lt_ref):
    half = out_ref.shape[0]
    span = 2 * half
    stats = msg_ref[:, heads * span : (heads + 1) * span, :]
    count = msg_ref.shape[0]
    scales, shifts, lse, lt = merge_weights([stats[i] for i in range(count)], heads)
    for head in range(heads):
        rows = slice(head * span, (head + 1) * span)
        merged = moved = 0.0
        for i, (scale, shift) in enumerate(zip(scales, shifts)):
            values = msg_ref[i, rows, :].astype(jnp.float32)
            merged += values * scale[:, head : head + 1]
            moved += values * shift[:, head : head + 1]
        cols = slice(head * HD, (head + 1) * HD)
        out_ref[:, cols] = merged[:half]
        out_tangent_ref[:, cols] = merged[half:] + moved[:half]
    lse_ref[...] = lse[:half, :heads]
    lt_ref[...] = lt[:half, :heads]


def merge(messages, heads):
    half = messages.shape[1] // (heads + 1) // 2
    vmem = pl.BlockSpec(memory_space=pltpu.VMEM)
    wide = jax.ShapeDtypeStruct((half, heads * HD), jnp.float32)
    small = jax.ShapeDtypeStruct((half, heads), jnp.float32)
    attended, attended_tangent, lse, lse_tangent = pl.pallas_call(
        lambda *refs: merge_kernel(heads, *refs),
        out_shape=(wide, wide, small, small),
        in_specs=[vmem],
        out_specs=(vmem,) * 4,
        compiler_params=pltpu.CompilerParams(vmem_limit_bytes=VMEM_LIMIT),
    )(messages)
    return attended, attended_tangent, lse.T, lse_tangent.T


def shift(array, step):
    count = lax.axis_size("y")
    return lax.ppermute(array, "y", [(i, (i + step) % count) for i in range(count)])


def per_device(query, query_tangent, keys, values, key_tangent, value_tangent):
    own = (keys, values, key_tangent, value_tangent)
    owners = lax.axis_size("z")
    heads = keys.shape[1] // HD
    row = jnp.concatenate([query, query_tangent], axis=0)
    row = spread(row, owners, lax.axis_size("x"))
    row, own = lax.optimization_barrier((row, own))
    other = tuple(lax.ppermute(array, "core", [(0, 1), (1, 0)]) for array in own)
    window = lax.all_to_all(row, ("z", "x"), split_axis=0, concat_axis=0, tiled=True)
    window = jnp.transpose(window, (1, 0, 2))
    window, other = lax.optimization_barrier((window, other))
    splits = (FIRST_HEADS, heads - FIRST_HEADS)
    steps = (1, 3, 2)
    windows = []
    first = 0
    for count in splits:
        part = window[:, :, first * HD : (first + count) * HD]
        windows.append([part] + [shift(part, step) for step in steps])
        first += count
    parts = []
    carried = ()
    first = 0
    for i, count in enumerate(splits):
        last = i == len(splits) - 1
        messages, carried = attend(windows[i], own, other, owners, first, last, carried)
        parts.append([messages[0]] + [shift(m, -step) for m, step in zip(messages[1:], steps)])
        first += count
    message = merge_group(parts, splits)
    message = lax.all_to_all(message, "z", split_axis=0, concat_axis=0, tiled=True)
    return merge(message, heads)


def solution(mesh):
    seq, head = mesh.devices.shape
    devices = mesh.devices.reshape(seq // (Y * CORES), Y, CORES, head)
    seq_axes = ("z", "y", "core")
    return jax.shard_map(
        per_device,
        mesh=Mesh(devices, (*seq_axes, "x")),
        in_specs=(P((*seq_axes, "x"), None),) * 2 + (P(seq_axes, "x"),) * 4,
        out_specs=(P(seq_axes, "x"),) * 2 + (P("x", seq_axes),) * 2,
        check_vma=False,
    )
```

```python
import math

import jax
import jax.numpy as jnp
from jax import lax
from jax.experimental import pallas as pl
from jax.experimental.pallas import tpu as pltpu
from jax.sharding import Mesh, PartitionSpec as P

HD = 128
LANES = 128
CORES = 2
Y = 4
ORDER = (4, 5, 6, 7, 0, 1, 2, 3)
NT = (((1,), (1,)), ((), ()))
VMEM_LIMIT = 32 * 1024 * 1024


def nt(a, b):
    return lax.dot_general(a, b, NT, preferred_element_type=jnp.float32)


def nn(a, b):
    return jnp.dot(a, b, preferred_element_type=jnp.float32)


def split3(x):
    hi = x.astype(jnp.bfloat16).astype(jnp.float32)
    mid = (x - hi).astype(jnp.bfloat16).astype(jnp.float32)
    return hi, mid, x - hi - mid


def encode(lse, lt, heads):
    total = None
    for i, part in enumerate((*split3(lse), *split3(lt))):
        part = pltpu.roll(part, i * heads, part.ndim - 1) if i else part
        total = part if total is None else total + part
    return total


def decode(stats, heads):
    parts = [
        pltpu.roll(stats, LANES - i * heads, stats.ndim - 1) if i else stats for i in range(6)
    ]
    return parts[2] + parts[1] + parts[0], parts[5] + parts[4] + parts[3]


def twice(x):
    return jnp.concatenate([x, x], axis=1)


def spread_kernel(copies, groups, row_ref, out_ref):
    width = row_ref.shape[1] // groups
    for group in range(groups):
        pair = row_ref[:, group * width : (group + 1) * width]
        for copy in range(copies):
            out_ref[copy * groups + group] = pair


def spread(row, copies, groups):
    arrays, width = row.shape
    vmem = pl.BlockSpec(memory_space=pltpu.VMEM)
    return pl.pallas_call(
        lambda *refs: spread_kernel(copies, groups, *refs),
        out_shape=jax.ShapeDtypeStruct((copies * groups, arrays, width // groups), row.dtype),
        in_specs=[vmem],
        out_specs=vmem,
        compiler_params=pltpu.CompilerParams(vmem_limit_bytes=VMEM_LIMIT),
    )(row)


LOADS = 2


def load_kernel(*refs):
    count = (len(refs) - 1) // 2
    sources, targets, sems = refs[:count], refs[count : 2 * count], refs[-1]
    copies = []
    for i, (source, target) in enumerate(zip(sources, targets)):
        rows = source.shape[0] // LOADS
        for j in range(LOADS):
            part = pl.ds(j * rows, rows)
            copies.append(
                pltpu.make_async_copy(source.at[part], target.at[part], sems.at[i * LOADS + j])
            )
    for copy in copies:
        copy.start()
    for copy in copies:
        copy.wait()


def load(arrays):
    count = len(arrays)
    size = sum(array.size for array in arrays)
    return pl.pallas_call(
        load_kernel,
        out_shape=[jax.ShapeDtypeStruct(array.shape, array.dtype) for array in arrays],
        in_specs=[pl.BlockSpec(memory_space=pl.ANY)] * count,
        out_specs=[pl.BlockSpec(memory_space=pltpu.VMEM)] * count,
        scratch_shapes=[pltpu.SemaphoreType.DMA((count * LOADS,))],
        compiler_params=pltpu.CompilerParams(vmem_limit_bytes=VMEM_LIMIT),
        cost_estimate=pl.CostEstimate(flops=0, bytes_accessed=4 * size, transcendentals=0),
    )(*arrays)


def blocks_of(refs):
    return refs[:4], refs[4:]


def attend_kernel(owners, groups, *refs):
    windows, keys, outs = refs[:groups], refs[groups : groups + 8], refs[groups + 8 :]
    rows = windows[0].shape[1]
    total_rows = rows * groups
    heads = windows[0].shape[2] // HD
    per_owner = rows // owners
    factor = 1.0 / math.sqrt(HD)
    power = factor * math.log2(math.e)
    lane = lax.broadcasted_iota(jnp.int32, (total_rows, LANES), 1)
    lses = jnp.zeros((total_rows, LANES), jnp.float32)
    lts = jnp.zeros((total_rows, LANES), jnp.float32)
    zeros = jnp.zeros((total_rows, HD), jnp.bfloat16)
    pending = None
    for head in range(heads):
        cols = slice(head * HD, (head + 1) * HD)
        q = jnp.concatenate([w[0, :, cols] for w in windows], axis=0)
        qt = jnp.concatenate([w[1, :, cols] for w in windows], axis=0)
        lhs = jnp.concatenate(
            [jnp.concatenate([q, zeros], axis=1), jnp.concatenate([qt, q], axis=1)], axis=0
        )
        scores, tangents, acc = [], [], 0.0
        for k, v, kt, vt in blocks_of(keys):
            both = nt(lhs, jnp.concatenate([k[:, cols], kt[:, cols]], axis=1))
            scores.append(both[:total_rows])
            tangents.append(both[total_rows:] * factor)
        top = jnp.max(jnp.maximum(scores[0], scores[1]), axis=1, keepdims=True)
        weights = [jnp.exp2((s - top) * power) for s in scores]
        products = [w * t for w, t in zip(weights, tangents)]
        total = jnp.sum(weights[0] + weights[1], axis=1, keepdims=True)
        slope = jnp.sum(products[0] + products[1], axis=1, keepdims=True)
        for w, p, (k, v, kt, vt) in zip(weights, products, blocks_of(keys)):
            both = jnp.concatenate([w.astype(jnp.bfloat16), p.astype(jnp.bfloat16)], axis=0)
            acc += nn(both, jnp.concatenate([v[:, cols], vt[:, cols]], axis=1))
        inverse = 1.0 / total
        lt = slope * inverse
        out = acc[:total_rows, :HD] * inverse
        out_tangent = (acc[total_rows:, :HD] + acc[:total_rows, HD:]) * inverse - lt * out
        lses = jnp.where(lane == head, top * factor + jnp.log(total), lses)
        lts = jnp.where(lane == head, lt, lts)
        tile = [
            x.reshape(groups * owners, per_owner, HD) for x in (out, out_tangent)
        ]
        if pending is None:
            pending = tile
            continue
        tile = [pending[0], tile[0], pending[1], tile[1]]
        tile = jnp.concatenate(tile, axis=1).astype(jnp.bfloat16)
        pending = None
        span = tile.shape[1]
        start = (head // 2) * span
        for i, ref in enumerate(outs):
            ref[:, start : start + span, :] = tile[i * owners : (i + 1) * owners]
    stats = twice(encode(lses, lts, heads).reshape(groups * owners, per_owner, LANES))
    span = stats.shape[1]
    for i, ref in enumerate(outs):
        part = stats[i * owners : (i + 1) * owners]
        ref[:, heads * span : (heads + 1) * span, :] = part.astype(jnp.bfloat16)


def attend(windows, own, other, owners):
    arrays, rows, width = windows[0].shape
    groups = len(windows)
    heads = width // HD
    message_rows = (heads + 1) * 2 * (rows // owners)
    vmem = pl.BlockSpec(memory_space=pltpu.VMEM)
    keys = own[0].shape[0] * 2
    return pl.pallas_call(
        lambda *refs: attend_kernel(owners, groups, *refs),
        out_shape=[jax.ShapeDtypeStruct((owners, message_rows, HD), jnp.bfloat16)] * groups,
        in_specs=[vmem] * (groups + 8),
        out_specs=[vmem] * groups,
        compiler_params=pltpu.CompilerParams(vmem_limit_bytes=VMEM_LIMIT),
        cost_estimate=pl.CostEstimate(
            flops=12 * rows * groups * keys * width,
            bytes_accessed=8 * keys * width,
            transcendentals=rows * groups * keys * heads,
        ),
    )(*windows, *own, *other)


def pairs(x):
    half = x.shape[-2] // 2
    row = lax.broadcasted_iota(jnp.int32, x.shape, x.ndim - 2)
    return jnp.where(row < half, x, pltpu.roll(x, LANES - 1, x.ndim - 1))


def merge_weights(stats, heads):
    decoded = [decode(s.astype(jnp.float32), heads) for s in stats]
    top = decoded[0][0]
    for lse, _ in decoded[1:]:
        top = jnp.maximum(top, lse)
    scales = [jnp.exp(lse - top) for lse, _ in decoded]
    total = sum(scales[1:], scales[0])
    inverse = 1.0 / total
    scales = [scale * inverse for scale in scales]
    lt = sum(scale * part for scale, (_, part) in zip(scales, decoded))
    shifts = [scale * (part - lt) for scale, (_, part) in zip(scales, decoded)]
    return [pairs(x) for x in scales], [pairs(x) for x in shifts], top + jnp.log(total), lt


def merge_group_kernel(heads, *refs):
    sources, out_ref = refs[:-1], refs[-1]
    owners, message_rows, _ = out_ref.shape
    span = message_rows // (heads + 1)
    scales, shifts, lse, lt = merge_weights(
        [ref[:, heads * span : (heads + 1) * span, :] for ref in sources], heads
    )
    for pair in range(heads // 2):
        head = 2 * pair
        start = head * span
        out = tangent = 0.0
        for ref, scale, shift in zip(sources, scales, shifts):
            values = ref[:, start : start + span, :].astype(jnp.float32)
            tangents = ref[:, start + span : start + 2 * span, :].astype(jnp.float32)
            scale = scale[:, :, head : head + 1]
            out += values * scale
            tangent += tangents * scale + values * shift[:, :, head : head + 1]
        tile = jnp.concatenate([out, tangent], axis=1).astype(jnp.bfloat16)
        for slot, owner in enumerate(ORDER):
            out_ref[slot, start : start + 2 * span, :] = tile[owner]
    lane = lax.broadcasted_iota(jnp.int32, lse.shape, 2)
    stats = encode(jnp.where(lane < heads, lse, 0.0), jnp.where(lane < heads, lt, 0.0), heads)
    stats = stats.astype(jnp.bfloat16)
    for slot, owner in enumerate(ORDER):
        out_ref[slot, heads * span : (heads + 1) * span, :] = stats[owner]


def merge_group(messages, heads):
    vmem = pl.BlockSpec(memory_space=pltpu.VMEM)
    return pl.pallas_call(
        lambda *refs: merge_group_kernel(heads, *refs),
        out_shape=jax.ShapeDtypeStruct(messages[0].shape, jnp.bfloat16),
        in_specs=[vmem] * len(messages),
        out_specs=vmem,
        compiler_params=pltpu.CompilerParams(vmem_limit_bytes=VMEM_LIMIT),
    )(*messages)


def merge_kernel(heads, msg_ref, out_ref, out_tangent_ref, lse_ref, lt_ref):
    half = out_ref.shape[0]
    span = 2 * half
    stats = msg_ref[:, heads * span : (heads + 1) * span, :]
    count = msg_ref.shape[0]
    scales, shifts, lse, lt = merge_weights([stats[i] for i in range(count)], heads)
    for head in range(0, heads, 2):
        start = head * span
        out = tangent = 0.0
        for i, (scale, shift) in enumerate(zip(scales, shifts)):
            values = msg_ref[i, start : start + span, :].astype(jnp.float32)
            tangents = msg_ref[i, start + span : start + 2 * span, :].astype(jnp.float32)
            scale = scale[:, head : head + 1]
            out += values * scale
            tangent += tangents * scale + values * shift[:, head : head + 1]
        for j in range(2):
            rows = slice(j * half, (j + 1) * half)
            cols = slice((head + j) * HD, (head + j + 1) * HD)
            out_ref[:, cols] = out[rows]
            out_tangent_ref[:, cols] = tangent[rows]
    lse_ref[...] = lse[:half, :heads]
    lt_ref[...] = lt[:half, :heads]


def merge(messages, heads):
    half = messages.shape[1] // (heads + 1) // 2
    vmem = pl.BlockSpec(memory_space=pltpu.VMEM)
    wide = jax.ShapeDtypeStruct((half, heads * HD), jnp.float32)
    small = jax.ShapeDtypeStruct((half, heads), jnp.float32)
    attended, attended_tangent, lse, lse_tangent = pl.pallas_call(
        lambda *refs: merge_kernel(heads, *refs),
        out_shape=(wide, wide, small, small),
        in_specs=[vmem],
        out_specs=(vmem,) * 4,
        compiler_params=pltpu.CompilerParams(vmem_limit_bytes=VMEM_LIMIT),
    )(messages)
    return attended, attended_tangent, lse.T, lse_tangent.T


def shift(array, step):
    count = lax.axis_size("y")
    return lax.ppermute(array, "y", [(i, (i + step) % count) for i in range(count)])


def per_device(query, query_tangent, keys, values, key_tangent, value_tangent):
    own = (keys, values, key_tangent, value_tangent)
    owners = lax.axis_size("z")
    heads = keys.shape[1] // HD
    row = jnp.concatenate([query, query_tangent], axis=0)
    row = spread(row, owners, lax.axis_size("x"))
    other = tuple(lax.ppermute(array, "core", [(0, 1), (1, 0)]) for array in own)
    window = lax.all_to_all(row, ("z", "x"), split_axis=0, concat_axis=0, tiled=True)
    window = jnp.transpose(window, (1, 0, 2))
    window, own, other = lax.optimization_barrier((window, own, other))
    own = load(own)
    steps = (2, 1, 3)
    windows = [window] + [shift(window, step) for step in steps]
    messages = attend(windows, own, other, owners)
    messages = [messages[0]] + [shift(m, -step) for m, step in zip(messages[1:], steps)]
    message = merge_group(messages, heads)
    message = lax.all_to_all(
        message, "z", split_axis=0, concat_axis=0, tiled=True, axis_index_groups=[list(ORDER)]
    )
    return merge(message, heads)


def solution(mesh):
    seq, head = mesh.devices.shape
    devices = mesh.devices.reshape(seq // (Y * CORES), Y, CORES, head)
    seq_axes = ("z", "y", "core")
    return jax.shard_map(
        per_device,
        mesh=Mesh(devices, (*seq_axes, "x")),
        in_specs=(P((*seq_axes, "x"), None),) * 2 + (P(seq_axes, "x"),) * 4,
        out_specs=(P(seq_axes, "x"),) * 2 + (P("x", seq_axes),) * 2,
        check_vma=False,
    )
```

```python
import math

import jax
import jax.numpy as jnp
from jax import lax
from jax.experimental import pallas as pl
from jax.experimental.pallas import tpu as pltpu
from jax.sharding import Mesh, PartitionSpec as P

HD = 128
LANES = 128
CORES = 2
Y = 4
ORDER = (4, 5, 6, 7, 0, 1, 2, 3)
NT = (((1,), (1,)), ((), ()))
VMEM_LIMIT = 32 * 1024 * 1024


def nt(a, b):
    return lax.dot_general(a, b, NT, preferred_element_type=jnp.float32)


def nn(a, b):
    return jnp.dot(a, b, preferred_element_type=jnp.float32)


def split3(x):
    hi = x.astype(jnp.bfloat16).astype(jnp.float32)
    mid = (x - hi).astype(jnp.bfloat16).astype(jnp.float32)
    return hi, mid, x - hi - mid


def encode(lse, lt, heads):
    total = None
    for i, part in enumerate((*split3(lse), *split3(lt))):
        part = pltpu.roll(part, i * heads, part.ndim - 1) if i else part
        total = part if total is None else total + part
    return total


def decode(stats, heads):
    parts = [
        pltpu.roll(stats, LANES - i * heads, stats.ndim - 1) if i else stats for i in range(6)
    ]
    return parts[2] + parts[1] + parts[0], parts[5] + parts[4] + parts[3]


def twice(x):
    return jnp.concatenate([x, x], axis=1)


def spread_kernel(copies, groups, row_ref, out_ref):
    width = row_ref.shape[1] // groups
    for group in range(groups):
        pair = row_ref[:, group * width : (group + 1) * width]
        for copy in range(copies):
            out_ref[copy * groups + group] = pair


def spread(row, copies, groups):
    arrays, width = row.shape
    vmem = pl.BlockSpec(memory_space=pltpu.VMEM)
    return pl.pallas_call(
        lambda *refs: spread_kernel(copies, groups, *refs),
        out_shape=jax.ShapeDtypeStruct((copies * groups, arrays, width // groups), row.dtype),
        in_specs=[vmem],
        out_specs=vmem,
        compiler_params=pltpu.CompilerParams(vmem_limit_bytes=VMEM_LIMIT),
    )(row)


LOADS = 2


def load_kernel(*refs):
    count = (len(refs) - 1) // 2
    sources, targets, sems = refs[:count], refs[count : 2 * count], refs[-1]
    copies = []
    for i, (source, target) in enumerate(zip(sources, targets)):
        rows = source.shape[0] // LOADS
        for j in range(LOADS):
            part = pl.ds(j * rows, rows)
            copies.append(
                pltpu.make_async_copy(source.at[part], target.at[part], sems.at[i * LOADS + j])
            )
    for copy in copies:
        copy.start()
    for copy in copies:
        copy.wait()


def load(arrays):
    count = len(arrays)
    size = sum(array.size for array in arrays)
    return pl.pallas_call(
        load_kernel,
        out_shape=[jax.ShapeDtypeStruct(array.shape, array.dtype) for array in arrays],
        in_specs=[pl.BlockSpec(memory_space=pl.ANY)] * count,
        out_specs=[pl.BlockSpec(memory_space=pltpu.VMEM)] * count,
        scratch_shapes=[pltpu.SemaphoreType.DMA((count * LOADS,))],
        compiler_params=pltpu.CompilerParams(vmem_limit_bytes=VMEM_LIMIT),
        cost_estimate=pl.CostEstimate(flops=0, bytes_accessed=4 * size, transcendentals=0),
    )(*arrays)


def blocks_of(refs):
    return refs[:4], refs[4:]


def attend_kernel(owners, groups, *refs):
    windows, keys, outs = refs[:groups], refs[groups : groups + 8], refs[groups + 8 :]
    rows = windows[0].shape[1]
    total_rows = rows * groups
    heads = windows[0].shape[2] // HD
    per_owner = rows // owners
    factor = 1.0 / math.sqrt(HD)
    power = factor * math.log2(math.e)
    lane = lax.broadcasted_iota(jnp.int32, (total_rows, LANES), 1)
    lses = jnp.zeros((total_rows, LANES), jnp.float32)
    lts = jnp.zeros((total_rows, LANES), jnp.float32)
    zeros = jnp.zeros((total_rows, HD), jnp.bfloat16)
    pending = None
    for head in range(heads):
        cols = slice(head * HD, (head + 1) * HD)
        q = jnp.concatenate([w[0, :, cols] for w in windows], axis=0)
        qt = jnp.concatenate([w[1, :, cols] for w in windows], axis=0)
        lhs = jnp.concatenate(
            [jnp.concatenate([q, zeros], axis=1), jnp.concatenate([qt, q], axis=1)], axis=0
        )
        scores, tangents, acc = [], [], 0.0
        for k, v, kt, vt in blocks_of(keys):
            both = nt(lhs, jnp.concatenate([k[:, cols], kt[:, cols]], axis=1))
            scores.append(both[:total_rows])
            tangents.append(both[total_rows:] * factor)
        top = jnp.max(jnp.maximum(scores[0], scores[1]), axis=1, keepdims=True)
        weights = [jnp.exp2((s - top) * power) for s in scores]
        products = [w * t for w, t in zip(weights, tangents)]
        total = jnp.sum(weights[0] + weights[1], axis=1, keepdims=True)
        slope = jnp.sum(products[0] + products[1], axis=1, keepdims=True)
        for w, p, (k, v, kt, vt) in zip(weights, products, blocks_of(keys)):
            both = jnp.concatenate([w.astype(jnp.bfloat16), p.astype(jnp.bfloat16)], axis=0)
            acc += nn(both, jnp.concatenate([v[:, cols], vt[:, cols]], axis=1))
        inverse = 1.0 / total
        lt = slope * inverse
        out = acc[:total_rows, :HD] * inverse
        out_tangent = (acc[total_rows:, :HD] + acc[:total_rows, HD:]) * inverse - lt * out
        lses = jnp.where(lane == head, top * factor + jnp.log(total), lses)
        lts = jnp.where(lane == head, lt, lts)
        tile = [
            x.reshape(groups * owners, per_owner, HD) for x in (out, out_tangent)
        ]
        if pending is None:
            pending = tile
            continue
        tile = [pending[0], tile[0], pending[1], tile[1]]
        tile = jnp.concatenate(tile, axis=1).astype(jnp.bfloat16)
        pending = None
        span = tile.shape[1]
        start = (head // 2) * span
        for i, ref in enumerate(outs):
            ref[:, start : start + span, :] = tile[i * owners : (i + 1) * owners]
    stats = twice(encode(lses, lts, heads).reshape(groups * owners, per_owner, LANES))
    span = stats.shape[1]
    for i, ref in enumerate(outs):
        part = stats[i * owners : (i + 1) * owners]
        ref[:, heads * span : (heads + 1) * span, :] = part.astype(jnp.bfloat16)


def attend(windows, own, other, owners):
    arrays, rows, width = windows[0].shape
    groups = len(windows)
    heads = width // HD
    message_rows = (heads + 1) * 2 * (rows // owners)
    vmem = pl.BlockSpec(memory_space=pltpu.VMEM)
    keys = own[0].shape[0] * 2
    return pl.pallas_call(
        lambda *refs: attend_kernel(owners, groups, *refs),
        out_shape=[jax.ShapeDtypeStruct((owners, message_rows, HD), jnp.bfloat16)] * groups,
        in_specs=[vmem] * (groups + 8),
        out_specs=[vmem] * groups,
        compiler_params=pltpu.CompilerParams(vmem_limit_bytes=VMEM_LIMIT),
        cost_estimate=pl.CostEstimate(
            flops=12 * rows * groups * keys * width,
            bytes_accessed=8 * keys * width,
            transcendentals=rows * groups * keys * heads,
        ),
    )(*windows, *own, *other)


def pairs(x):
    half = x.shape[-2] // 2
    row = lax.broadcasted_iota(jnp.int32, x.shape, x.ndim - 2)
    return jnp.where(row < half, x, pltpu.roll(x, LANES - 1, x.ndim - 1))


def merge_weights(stats, heads):
    decoded = [decode(s.astype(jnp.float32), heads) for s in stats]
    top = decoded[0][0]
    for lse, _ in decoded[1:]:
        top = jnp.maximum(top, lse)
    scales = [jnp.exp(lse - top) for lse, _ in decoded]
    total = sum(scales[1:], scales[0])
    inverse = 1.0 / total
    scales = [scale * inverse for scale in scales]
    lt = sum(scale * part for scale, (_, part) in zip(scales, decoded))
    shifts = [scale * (part - lt) for scale, (_, part) in zip(scales, decoded)]
    return [pairs(x) for x in scales], [pairs(x) for x in shifts], top + jnp.log(total), lt


def merge_group_kernel(heads, *refs):
    sources, out_ref = refs[:-1], refs[-1]
    owners, message_rows, _ = out_ref.shape
    span = message_rows // (heads + 1)
    scales, shifts, lse, lt = merge_weights(
        [ref[:, heads * span : (heads + 1) * span, :] for ref in sources], heads
    )
    for pair in range(heads // 2):
        head = 2 * pair
        start = head * span
        out = tangent = 0.0
        for ref, scale, shift in zip(sources, scales, shifts):
            block = ref[:, start : start + 2 * span, :].astype(jnp.float32)
            values, tangents = block[:, :span], block[:, span:]
            scale = scale[:, :, head : head + 1]
            out += values * scale
            tangent += tangents * scale + values * shift[:, :, head : head + 1]
        tile = jnp.concatenate([out, tangent], axis=1).astype(jnp.bfloat16)
        for slot, owner in enumerate(ORDER):
            out_ref[slot, start : start + 2 * span, :] = tile[owner]
    lane = lax.broadcasted_iota(jnp.int32, lse.shape, 2)
    stats = encode(jnp.where(lane < heads, lse, 0.0), jnp.where(lane < heads, lt, 0.0), heads)
    stats = stats.astype(jnp.bfloat16)
    for slot, owner in enumerate(ORDER):
        out_ref[slot, heads * span : (heads + 1) * span, :] = stats[owner]


def merge_group(messages, heads):
    vmem = pl.BlockSpec(memory_space=pltpu.VMEM)
    return pl.pallas_call(
        lambda *refs: merge_group_kernel(heads, *refs),
        out_shape=jax.ShapeDtypeStruct(messages[0].shape, jnp.bfloat16),
        in_specs=[vmem] * len(messages),
        out_specs=vmem,
        compiler_params=pltpu.CompilerParams(vmem_limit_bytes=VMEM_LIMIT),
    )(*messages)


def merge_kernel(heads, msg_ref, out_ref, out_tangent_ref, lse_ref, lt_ref):
    half = out_ref.shape[0]
    span = 2 * half
    stats = msg_ref[:, heads * span : (heads + 1) * span, :]
    count = msg_ref.shape[0]
    scales, shifts, lse, lt = merge_weights([stats[i] for i in range(count)], heads)
    for head in range(0, heads, 2):
        start = head * span
        out = tangent = 0.0
        for i, (scale, shift) in enumerate(zip(scales, shifts)):
            block = msg_ref[i, start : start + 2 * span, :].astype(jnp.float32)
            values, tangents = block[:span], block[span:]
            scale = scale[:, head : head + 1]
            out += values * scale
            tangent += tangents * scale + values * shift[:, head : head + 1]
        for j in range(2):
            rows = slice(j * half, (j + 1) * half)
            cols = slice((head + j) * HD, (head + j + 1) * HD)
            out_ref[:, cols] = out[rows]
            out_tangent_ref[:, cols] = tangent[rows]
    lse_ref[...] = lse[:half, :heads]
    lt_ref[...] = lt[:half, :heads]


def merge(messages, heads):
    half = messages.shape[1] // (heads + 1) // 2
    vmem = pl.BlockSpec(memory_space=pltpu.VMEM)
    wide = jax.ShapeDtypeStruct((half, heads * HD), jnp.float32)
    small = jax.ShapeDtypeStruct((half, heads), jnp.float32)
    attended, attended_tangent, lse, lse_tangent = pl.pallas_call(
        lambda *refs: merge_kernel(heads, *refs),
        out_shape=(wide, wide, small, small),
        in_specs=[vmem],
        out_specs=(vmem,) * 4,
        compiler_params=pltpu.CompilerParams(vmem_limit_bytes=VMEM_LIMIT),
    )(messages)
    return attended, attended_tangent, lse.T, lse_tangent.T


def shift(array, step):
    count = lax.axis_size("y")
    return lax.ppermute(array, "y", [(i, (i + step) % count) for i in range(count)])


def per_device(query, query_tangent, keys, values, key_tangent, value_tangent):
    own = (keys, values, key_tangent, value_tangent)
    owners = lax.axis_size("z")
    heads = keys.shape[1] // HD
    row = jnp.concatenate([query, query_tangent], axis=0)
    row = spread(row, owners, lax.axis_size("x"))
    other = tuple(lax.ppermute(array, "core", [(0, 1), (1, 0)]) for array in own)
    window = lax.all_to_all(row, ("z", "x"), split_axis=0, concat_axis=0, tiled=True)
    window = jnp.transpose(window, (1, 0, 2))
    window, own, other = lax.optimization_barrier((window, own, other))
    own = load(own)
    steps = (2, 1, 3)
    windows = [window] + [shift(window, step) for step in steps]
    messages = attend(windows, own, other, owners)
    messages = [messages[0]] + [shift(m, -step) for m, step in zip(messages[1:], steps)]
    message = merge_group(messages, heads)
    message = lax.all_to_all(
        message, "z", split_axis=0, concat_axis=0, tiled=True, axis_index_groups=[list(ORDER)]
    )
    return merge(message, heads)


def solution(mesh):
    seq, head = mesh.devices.shape
    devices = mesh.devices.reshape(seq // (Y * CORES), Y, CORES, head)
    seq_axes = ("z", "y", "core")
    return jax.shard_map(
        per_device,
        mesh=Mesh(devices, (*seq_axes, "x")),
        in_specs=(P((*seq_axes, "x"), None),) * 2 + (P(seq_axes, "x"),) * 4,
        out_specs=(P(seq_axes, "x"),) * 2 + (P("x", seq_axes),) * 2,
        check_vma=False,
    )
```

```python
import math

import jax
import jax.numpy as jnp
from jax import lax
from jax.experimental import pallas as pl
from jax.experimental.pallas import tpu as pltpu
from jax.sharding import Mesh, PartitionSpec as P

HD = 128
LANES = 128
CORES = 2
Y = 4
ORDER = (4, 5, 6, 7, 0, 1, 2, 3)
NT = (((1,), (1,)), ((), ()))
VMEM_LIMIT = 32 * 1024 * 1024


def nt(a, b):
    return lax.dot_general(a, b, NT, preferred_element_type=jnp.float32)


def nn(a, b):
    return jnp.dot(a, b, preferred_element_type=jnp.float32)


def split3(x):
    hi = x.astype(jnp.bfloat16).astype(jnp.float32)
    mid = (x - hi).astype(jnp.bfloat16).astype(jnp.float32)
    return hi, mid, x - hi - mid


def encode(lse, lt, heads):
    total = None
    for i, part in enumerate((*split3(lse), *split3(lt))):
        part = pltpu.roll(part, i * heads, part.ndim - 1) if i else part
        total = part if total is None else total + part
    return total


def decode(stats, heads):
    parts = [
        pltpu.roll(stats, LANES - i * heads, stats.ndim - 1) if i else stats for i in range(6)
    ]
    return parts[2] + parts[1] + parts[0], parts[5] + parts[4] + parts[3]


def twice(x):
    return jnp.concatenate([x, x], axis=1)


def spread_kernel(copies, groups, row_ref, out_ref):
    width = row_ref.shape[1] // groups
    for group in range(groups):
        pair = row_ref[:, group * width : (group + 1) * width]
        for copy in range(copies):
            out_ref[copy * groups + group] = pair


def spread(row, copies, groups):
    arrays, width = row.shape
    vmem = pl.BlockSpec(memory_space=pltpu.VMEM)
    return pl.pallas_call(
        lambda *refs: spread_kernel(copies, groups, *refs),
        out_shape=jax.ShapeDtypeStruct((copies * groups, arrays, width // groups), row.dtype),
        in_specs=[vmem],
        out_specs=vmem,
        compiler_params=pltpu.CompilerParams(vmem_limit_bytes=VMEM_LIMIT),
    )(row)


LOADS = 2


def load_kernel(*refs):
    count = (len(refs) - 1) // 2
    sources, targets, sems = refs[:count], refs[count : 2 * count], refs[-1]
    copies = []
    for i, (source, target) in enumerate(zip(sources, targets)):
        rows = source.shape[0] // LOADS
        for j in range(LOADS):
            part = pl.ds(j * rows, rows)
            copies.append(
                pltpu.make_async_copy(source.at[part], target.at[part], sems.at[i * LOADS + j])
            )
    for copy in copies:
        copy.start()
    for copy in copies:
        copy.wait()


def load(arrays):
    count = len(arrays)
    size = sum(array.size for array in arrays)
    return pl.pallas_call(
        load_kernel,
        out_shape=[jax.ShapeDtypeStruct(array.shape, array.dtype) for array in arrays],
        in_specs=[pl.BlockSpec(memory_space=pl.ANY)] * count,
        out_specs=[pl.BlockSpec(memory_space=pltpu.VMEM)] * count,
        scratch_shapes=[pltpu.SemaphoreType.DMA((count * LOADS,))],
        compiler_params=pltpu.CompilerParams(vmem_limit_bytes=VMEM_LIMIT),
        cost_estimate=pl.CostEstimate(flops=0, bytes_accessed=4 * size, transcendentals=0),
    )(*arrays)


def blocks_of(refs):
    return refs[:4], refs[4:]


def attend_kernel(owners, groups, *refs):
    windows, keys, outs = refs[:groups], refs[groups : groups + 8], refs[groups + 8 :]
    rows = windows[0].shape[1]
    total_rows = rows * groups
    heads = windows[0].shape[2] // HD
    per_owner = rows // owners
    factor = 1.0 / math.sqrt(HD)
    power = factor * math.log2(math.e)
    lane = lax.broadcasted_iota(jnp.int32, (total_rows, LANES), 1)
    lses = jnp.zeros((total_rows, LANES), jnp.float32)
    lts = jnp.zeros((total_rows, LANES), jnp.float32)
    zeros = jnp.zeros((total_rows, HD), jnp.bfloat16)
    pending = None
    for head in range(heads):
        cols = slice(head * HD, (head + 1) * HD)
        q = jnp.concatenate([w[0, :, cols] for w in windows], axis=0)
        qt = jnp.concatenate([w[1, :, cols] for w in windows], axis=0)
        lhs = jnp.concatenate(
            [jnp.concatenate([q, zeros], axis=1), jnp.concatenate([qt, q], axis=1)], axis=0
        )
        scores, tangents, acc = [], [], 0.0
        for k, v, kt, vt in blocks_of(keys):
            both = nt(lhs, jnp.concatenate([k[:, cols], kt[:, cols]], axis=1))
            scores.append(both[:total_rows])
            tangents.append(both[total_rows:] * factor)
        top = jnp.max(jnp.maximum(scores[0], scores[1]), axis=1, keepdims=True)
        weights = [jnp.exp2((s - top) * power) for s in scores]
        products = [w * t for w, t in zip(weights, tangents)]
        total = jnp.sum(weights[0] + weights[1], axis=1, keepdims=True)
        slope = jnp.sum(products[0] + products[1], axis=1, keepdims=True)
        for w, p, (k, v, kt, vt) in zip(weights, products, blocks_of(keys)):
            both = jnp.concatenate([w.astype(jnp.bfloat16), p.astype(jnp.bfloat16)], axis=0)
            acc += nn(both, jnp.concatenate([v[:, cols], vt[:, cols]], axis=1))
        inverse = 1.0 / total
        lt = slope * inverse
        out = acc[:total_rows, :HD] * inverse
        out_tangent = (acc[total_rows:, :HD] + acc[:total_rows, HD:]) * inverse - lt * out
        lses = jnp.where(lane == head, top * factor + jnp.log(total), lses)
        lts = jnp.where(lane == head, lt, lts)
        tile = [
            x.reshape(groups * owners, per_owner, HD) for x in (out, out_tangent)
        ]
        if pending is None:
            pending = tile
            continue
        tile = [pending[0], tile[0], pending[1], tile[1]]
        tile = jnp.concatenate(tile, axis=1).astype(jnp.bfloat16)
        pending = None
        span = tile.shape[1]
        start = (head // 2) * span
        rows_each = heads * span // 2
        for i, ref in enumerate(outs):
            for owner in range(owners):
                place = owner * rows_each + start
                ref[place : place + span, :] = tile[i * owners + owner]
    stats = encode(lses, lts, heads).astype(jnp.bfloat16)
    for i, ref in enumerate(outs):
        ref[ref.shape[0] - rows :, :] = stats[i * rows : (i + 1) * rows]


def attend(windows, own, other, owners):
    arrays, rows, width = windows[0].shape
    groups = len(windows)
    heads = width // HD
    message_rows = (2 * heads + 1) * rows
    vmem = pl.BlockSpec(memory_space=pltpu.VMEM)
    keys = own[0].shape[0] * 2
    return pl.pallas_call(
        lambda *refs: attend_kernel(owners, groups, *refs),
        out_shape=[jax.ShapeDtypeStruct((message_rows, HD), jnp.bfloat16)] * groups,
        in_specs=[vmem] * (groups + 8),
        out_specs=[vmem] * groups,
        compiler_params=pltpu.CompilerParams(vmem_limit_bytes=VMEM_LIMIT),
        cost_estimate=pl.CostEstimate(
            flops=12 * rows * groups * keys * width,
            bytes_accessed=8 * keys * width,
            transcendentals=rows * groups * keys * heads,
        ),
    )(*windows, *own, *other)


def pairs(x):
    half = x.shape[-2] // 2
    row = lax.broadcasted_iota(jnp.int32, x.shape, x.ndim - 2)
    return jnp.where(row < half, x, pltpu.roll(x, LANES - 1, x.ndim - 1))


def merge_weights(stats, heads):
    decoded = [decode(s.astype(jnp.float32), heads) for s in stats]
    top = decoded[0][0]
    for lse, _ in decoded[1:]:
        top = jnp.maximum(top, lse)
    scales = [jnp.exp(lse - top) for lse, _ in decoded]
    total = sum(scales[1:], scales[0])
    inverse = 1.0 / total
    scales = [scale * inverse for scale in scales]
    lt = sum(scale * part for scale, (_, part) in zip(scales, decoded))
    shifts = [scale * (part - lt) for scale, (_, part) in zip(scales, decoded)]
    return [pairs(x) for x in scales], [pairs(x) for x in shifts], top + jnp.log(total), lt


def merge_group_kernel(heads, *refs):
    sources, out_ref = refs[:-1], refs[-1]
    owners, message_rows, _ = out_ref.shape
    span = message_rows // (heads + 1)
    rows_each = heads * span
    stats = [ref[owners * rows_each :, :].astype(jnp.float32) for ref in sources]
    scales, shifts, lse, lt = merge_weights(
        [twice(x.reshape(owners, span // 2, LANES)) for x in stats], heads
    )
    for pair in range(heads // 2):
        head = 2 * pair
        start = head * span
        out = tangent = 0.0
        for ref, scale, shift in zip(sources, scales, shifts):
            places = [owner * rows_each + start for owner in range(owners)]
            block = jnp.stack([ref[place : place + 2 * span, :] for place in places])
            block = block.astype(jnp.float32)
            values, tangents = block[:, :span], block[:, span:]
            scale = scale[:, :, head : head + 1]
            out += values * scale
            tangent += tangents * scale + values * shift[:, :, head : head + 1]
        tile = jnp.concatenate([out, tangent], axis=1).astype(jnp.bfloat16)
        for slot, owner in enumerate(ORDER):
            out_ref[slot, start : start + 2 * span, :] = tile[owner]
    lane = lax.broadcasted_iota(jnp.int32, lse.shape, 2)
    stats = encode(jnp.where(lane < heads, lse, 0.0), jnp.where(lane < heads, lt, 0.0), heads)
    stats = stats.astype(jnp.bfloat16)
    for slot, owner in enumerate(ORDER):
        out_ref[slot, heads * span : (heads + 1) * span, :] = stats[owner]


def merge_group(messages, heads, owners):
    vmem = pl.BlockSpec(memory_space=pltpu.VMEM)
    rows = messages[0].shape[0] // owners // (2 * heads + 1) * 2 * (heads + 1)
    return pl.pallas_call(
        lambda *refs: merge_group_kernel(heads, *refs),
        out_shape=jax.ShapeDtypeStruct((owners, rows, HD), jnp.bfloat16),
        in_specs=[vmem] * len(messages),
        out_specs=vmem,
        compiler_params=pltpu.CompilerParams(vmem_limit_bytes=VMEM_LIMIT),
    )(*messages)


def merge_kernel(heads, msg_ref, out_ref, out_tangent_ref, lse_ref, lt_ref):
    half = out_ref.shape[0]
    span = 2 * half
    stats = msg_ref[:, heads * span : (heads + 1) * span, :]
    count = msg_ref.shape[0]
    scales, shifts, lse, lt = merge_weights([stats[i] for i in range(count)], heads)
    for head in range(0, heads, 2):
        start = head * span
        out = tangent = 0.0
        for i, (scale, shift) in enumerate(zip(scales, shifts)):
            block = msg_ref[i, start : start + 2 * span, :].astype(jnp.float32)
            values, tangents = block[:span], block[span:]
            scale = scale[:, head : head + 1]
            out += values * scale
            tangent += tangents * scale + values * shift[:, head : head + 1]
        for j in range(2):
            rows = slice(j * half, (j + 1) * half)
            cols = slice((head + j) * HD, (head + j + 1) * HD)
            out_ref[:, cols] = out[rows]
            out_tangent_ref[:, cols] = tangent[rows]
    lse_ref[...] = lse[:half, :heads]
    lt_ref[...] = lt[:half, :heads]


def merge(messages, heads):
    half = messages.shape[1] // (heads + 1) // 2
    vmem = pl.BlockSpec(memory_space=pltpu.VMEM)
    wide = jax.ShapeDtypeStruct((half, heads * HD), jnp.float32)
    small = jax.ShapeDtypeStruct((half, heads), jnp.float32)
    attended, attended_tangent, lse, lse_tangent = pl.pallas_call(
        lambda *refs: merge_kernel(heads, *refs),
        out_shape=(wide, wide, small, small),
        in_specs=[vmem],
        out_specs=(vmem,) * 4,
        compiler_params=pltpu.CompilerParams(vmem_limit_bytes=VMEM_LIMIT),
    )(messages)
    return attended, attended_tangent, lse.T, lse_tangent.T


def shift(array, step):
    count = lax.axis_size("y")
    return lax.ppermute(array, "y", [(i, (i + step) % count) for i in range(count)])


def per_device(query, query_tangent, keys, values, key_tangent, value_tangent):
    own = (keys, values, key_tangent, value_tangent)
    owners = lax.axis_size("z")
    heads = keys.shape[1] // HD
    row = jnp.concatenate([query, query_tangent], axis=0)
    row = spread(row, owners, lax.axis_size("x"))
    other = tuple(lax.ppermute(array, "core", [(0, 1), (1, 0)]) for array in own)
    window = lax.all_to_all(row, ("z", "x"), split_axis=0, concat_axis=0, tiled=True)
    window = jnp.transpose(window, (1, 0, 2))
    window, own, other = lax.optimization_barrier((window, own, other))
    own = load(own)
    steps = (2, 1, 3)
    windows = [window] + [shift(window, step) for step in steps]
    messages = attend(windows, own, other, owners)
    messages = [messages[0]] + [shift(m, -step) for m, step in zip(messages[1:], steps)]
    message = merge_group(messages, heads, owners)
    message = lax.all_to_all(
        message, "z", split_axis=0, concat_axis=0, tiled=True, axis_index_groups=[list(ORDER)]
    )
    return merge(message, heads)


def solution(mesh):
    seq, head = mesh.devices.shape
    devices = mesh.devices.reshape(seq // (Y * CORES), Y, CORES, head)
    seq_axes = ("z", "y", "core")
    return jax.shard_map(
        per_device,
        mesh=Mesh(devices, (*seq_axes, "x")),
        in_specs=(P((*seq_axes, "x"), None),) * 2 + (P(seq_axes, "x"),) * 4,
        out_specs=(P(seq_axes, "x"),) * 2 + (P("x", seq_axes),) * 2,
        check_vma=False,
    )
```
